32 devices in a mesh: dom: 32 (over z, y, x, core).
Axes of the slice: x: 2, y: 2, z: 4, core: 2. Of those that a mesh axis runs over, the one named last changes fastest.
Arguments:
- right_side: float32 [64, 4096], P(None, 'dom'), may hold values from -8 to 8
- sigma: float32 [64, 4096], P(None, 'dom'), may hold values from 0.5 to 2
- reluctivity: float32 [64, 4096], P(None, 'dom'), may hold values from 0.2 to 5
- curl_blocks: float32 [6, 64, 64, 4096], P(None, None, None, 'dom'), may hold values from -0.3125 to 0.3125
- pattern: int32 [6, 4096], P(None, 'dom'), may hold values from 0 to 191
- cond_weight: float32 [64, 16384], P(None, 'dom'), may hold values from -0.25 to 0.25
- cond_block: int32 [16384], P('dom'), may hold values from 0 to 127
- cond_coil: int32 [16384, 1], P('dom'), may hold values from 0 to 83; in each aligned block of 512 rows (0 to 511, 512 to 1023, ...) at most 16 rows name the same one
- coil_phase: int32 [84], replicated, may hold values from 0 to 3
- coil_resistance: float32 [84], replicated, may hold values from 0.5 to 2
- switch_state: int32 [3], replicated, may hold values from 0 to 1
Outputs:
- solution_field: float32 [64, 4096], P(None, 'dom')
- residual: float32 [64, 4096], P(None, 'dom')
The draws below stay inside these ranges and needn't reach their ends.
Inputs may be any that keep to these rules, and one draw needn't show every extreme that they name: `cond_coil`: no coil is named by more than 16 of one partition's 512 conductor rows, a bound that some block reaches.
All inputs are finite; a program needn't handle non-finite values.
Results may differ from the reference program's by a relative error of at most 0.00055.
Values sent between devices are 32-bit elements; how exact they have to be, the bound alone decides.
A program may use at most 64 MiB of HBM per device.

```python
import math
import jax
import jax.numpy as jnp
import numpy as np
from jax import lax

BS = 64
KB = 6
NB = 128
HALO = 32
BLOCKS = 4096
NC = 512
CAP = 16
COND = 16384
NCOIL = 84
NPH = 3
ITERS = 3
N_DOM = 32


def with_ends(array, rng, least, largest):
    shape = array.shape
    index_at = [jax.random.randint(jax.random.fold_in(rng, axis), (), 0, shape[axis]) for axis in range(len(shape))]
    array = array.at[tuple(index_at)].set(least)
    longest = shape.index(max(shape))
    index_at[longest] = (index_at[longest] + 1) % shape[longest]
    return array.at[tuple(index_at)].set(largest)


def levels(key, extent, cuts, least, largest):
    gain = 1.0
    for dim, shards_of in cuts:
        heights = jax.random.uniform(jax.random.fold_in(jax.random.fold_in(key, 6), dim), (shards_of,), jnp.float32, least / len(cuts), largest / len(cuts))
        gain = gain * jnp.repeat(jnp.exp(heights), extent[dim] // shards_of).reshape((-1,) + (1,) * (len(extent) - 1 - dim))
    return gain


def assign_block(rng, own, number, rows, count, top, bound, skew):
    sequence = jax.random.permutation(rng, count)
    packed, usual = load_shares(count, rows * top, bound, skew, True), load_shares(count, rows * top, bound, skew, False)
    places = jnp.arange(count)

    def named(tallies, rotation):
        used = int((tallies > 0).sum())
        fixed = max(1, used // 4)
        shifted = fixed + (places - fixed + rotation * (used - fixed)) % max(1, count - fixed)
        return jnp.zeros((count,), jnp.int32).at[sequence[jnp.where(places < fixed, places, shifted)]].set(jnp.asarray(tallies, jnp.int32))

    tallies = jnp.where(number % 4 == 0, named(packed, number // 4), named(usual, number - number // 4 - 1))
    mixed = jax.random.permutation(jax.random.fold_in(own, 3), count)
    donor, sink = mixed[0:count // 2 * 2:2], mixed[1:count // 2 * 2:2]
    slack = jnp.minimum(tallies[donor] - 1, bound - tallies[sink]) // 2
    slack = jnp.where((donor == sequence[0]) | (sink == sequence[0]) | (tallies[sink] == 0), 0, jnp.maximum(slack, 0))
    shifted = jax.random.randint(jax.random.fold_in(own, 4), (count // 2,), 0, 1 << 20) % (slack + 1)
    tallies = tallies.at[donor].add(-shifted).at[sink].add(shifted)
    labels = jnp.searchsorted(jnp.cumsum(tallies), jnp.arange(rows * top), side="right").astype(jnp.int32)
    grid = labels.reshape(top, rows).T
    grid = grid[jax.random.permutation(jax.random.fold_in(own, 1), rows)]
    rotation = jax.random.randint(jax.random.fold_in(own, 2), (rows, 1), 0, top)
    return jnp.take_along_axis(grid, (jnp.arange(top)[None, :] + rotation) % top, axis=1)


def load_shares(amount, total, most, lean, full):
    portions = [(1 << 20) // math.isqrt(rank ** lean) + 1 for rank in range(1, amount + 1)]
    largest = most if full else min(most, max(-(-total // amount), total * portions[0] // sum(portions)))
    least = 1 if total - largest >= amount - 1 else 0
    counts, spare = [largest] + [least] * (amount - 1), total - largest - least * (amount - 1)
    while spare > 0:
        free = [i for i in range(1, amount) if counts[i] < largest] or [i for i in range(1, amount) if counts[i] < most]
        whole, budget = sum([portions[i] for i in free]), spare
        for i in free:
            more = min(most - counts[i], max(1, budget * portions[i] // whole), spare)
            counts[i] = counts[i] + more
            spare = spare - more
    return np.array(counts)


def noise(own_key, shape, scale, limit, split=(), kind=jnp.bfloat16):
    values = scale * jax.random.normal(own_key, shape, jnp.float32)
    if split:
        values = values * levels(own_key, shape, split, -0.22, 0.18)
    return jnp.clip(values, -limit, limit).astype(kind)


def setup_inputs(seed: int = 0) -> dict:
    seeds = jax.random.split(jax.random.key(seed), 12)
    right_side = noise(seeds[0], (BS, BLOCKS), 1.0, 8.0, ((1, 32),), jnp.float32)
    sigma = jnp.clip(jnp.exp(math.log(2.0) - 1.3862944 * jax.random.uniform(seeds[1], (BS, BLOCKS), jnp.float32) ** levels(seeds[1], (BS, BLOCKS), ((1, 32),), -0.2, 0.2)), 0.5, 2.0)
    reluctivity = jnp.clip(jnp.exp(math.log(5.0) - 3.218876 * jax.random.uniform(seeds[2], (BS, BLOCKS), jnp.float32) ** levels(seeds[2], (BS, BLOCKS), ((1, 32),), -0.2, 0.2)), 0.2, 5.0)
    curl_blocks = noise(seeds[3], (KB, BS, BS, BLOCKS), (BS * KB) ** -0.5, 0.3125, ((3, 32),), jnp.float32)
    pattern = with_ends(jax.random.randint(seeds[4], (KB, BLOCKS), 0, NB + 2 * HALO), jax.random.fold_in(seeds[4], 1), 0, (NB + 2 * HALO) - 1).astype(jnp.int32)
    cond_weight = noise(seeds[5], (BS, COND), (COND * 16 // (5 * NCOIL)) ** -0.5, 0.25, ((1, 32),), jnp.float32)
    cond_block = with_ends(jax.random.randint(seeds[6], (COND,), 0, NB), jax.random.fold_in(seeds[6], 1), 0, NB - 1).astype(jnp.int32)
    cond_coil_keys = jax.random.split(jax.random.fold_in(seeds[7], 1), COND // NC)
    cond_coil_turns = jax.random.permutation(jax.random.fold_in(seeds[7], 3), COND // NC)
    cond_coil = jax.vmap(lambda own, number: assign_block(jax.random.fold_in(seeds[7], 2), own, number, NC, NCOIL, 1, CAP, 2))(cond_coil_keys, cond_coil_turns).reshape((COND, 1))
    coil_phase = with_ends(jax.random.randint(seeds[8], (NCOIL,), 0, NPH + 1), jax.random.fold_in(seeds[8], 1), 0, NPH).astype(jnp.int32)
    coil_resistance = jnp.clip(jnp.exp(jax.random.uniform(seeds[9], (NCOIL,), jnp.float32, math.log(0.5), math.log(2.0))), 0.5, 2.0)
    switch_state = jax.random.randint(seeds[10], (NPH,), 0, 2).astype(jnp.int32)
    return {"right_side": right_side, "sigma": sigma, "reluctivity": reluctivity, "curl_blocks": curl_blocks, "pattern": pattern, "cond_weight": cond_weight, "cond_block": cond_block, "cond_coil": cond_coil, "coil_phase": coil_phase, "coil_resistance": coil_resistance, "switch_state": switch_state}


link_scale = 16.0


def reference(right_side, sigma, reluctivity, curl_blocks, pattern, cond_weight, cond_block, cond_coil, coil_phase, coil_resistance, switch_state):
    width = right_side.shape[0]
    total_blocks = right_side.shape[1]
    block_count = total_blocks // N_DOM
    halo_width = block_count // 4
    row_total = cond_block.shape[0]
    row_count = row_total // N_DOM
    coil_rows = cond_coil[:, 0]
    gblock = (cond_block + (jnp.arange(row_total, dtype=jnp.int32) // row_count) * block_count).astype(jnp.int32)
    switch_float = switch_state.astype(jnp.float32)
    table = jnp.concatenate([switch_float - jnp.mean(switch_float), jnp.zeros((1,), jnp.float32)])
    coil_volts = link_scale * table[coil_phase]
    row_source = (coil_volts / coil_resistance)[coil_rows]
    rhs = right_side + jnp.zeros_like(right_side).at[:, gblock].add(cond_weight * row_source[None, :])

    def operate(field):
        padded = jnp.pad(field, ((0, 0), (halo_width, halo_width)))

        def one_part(domain):
            start = (domain * block_count).astype(jnp.int32)
            window = lax.dynamic_slice_in_dim(padded, start, block_count + 2 * halo_width, 1)
            blocks = lax.dynamic_slice_in_dim(curl_blocks, start, block_count, 3)
            columns = lax.dynamic_slice_in_dim(pattern, start, block_count, 1)
            weights = lax.dynamic_slice_in_dim(reluctivity, start, block_count, 1)
            picked = window[:, columns]
            face_flux = jnp.einsum("kabn,bkn->an", blocks, picked, precision=lax.Precision.HIGHEST)
            back_terms = jnp.einsum("kabn,an->bkn", blocks, weights * face_flux, precision=lax.Precision.HIGHEST)
            return jnp.zeros_like(window).at[:, columns].add(back_terms)

        spreads = lax.map(one_part, jnp.arange(N_DOM, dtype=jnp.int32))
        centre = spreads[:, :, halo_width:halo_width + block_count]
        left_rims = spreads[:, :, :halo_width]
        right_rims = spreads[:, :, halo_width + block_count:]
        centre = centre.at[:-1, :, block_count - halo_width:].add(left_rims[1:])
        centre = centre.at[1:, :, :halo_width].add(right_rims[:-1])
        back_field = jnp.transpose(centre, (1, 0, 2)).reshape(width, total_blocks)
        partial_link = jnp.sum(cond_weight * field[:, gblock], axis=0)
        linkage = jnp.zeros((coil_resistance.shape[0],), jnp.float32).at[coil_rows].add(partial_link)
        currents = linkage / coil_resistance
        coupled = jnp.zeros_like(field).at[:, gblock].add(cond_weight * currents[coil_rows][None, :])
        return sigma * field + back_field + coupled

    solution_field = jnp.zeros_like(rhs)
    residual, direction = rhs, rhs
    norm_now = jnp.sum(residual * residual)
    for turn_index in range(ITERS):
        image = operate(direction)
        alpha = norm_now / jnp.sum(direction * image)
        solution_field = solution_field + alpha * direction
        residual = residual - alpha * image
        norm_next = jnp.sum(residual * residual)
        direction = residual + (norm_next / norm_now) * direction
        norm_now = norm_next
    return solution_field, residual
```

```python
import functools

import jax
import jax.numpy as jnp
from jax import lax
from jax.experimental import pallas as pl
from jax.experimental.pallas import tpu as pltpu
from jax.sharding import PartitionSpec as P

ITERS = 3
LINK_SCALE = 16.0
LANES = 128
RR_ROW = 126
RAR_ROW = 127
MESH = pl.DeviceIdType.MESH
F32 = jnp.float32
BF16 = jnp.bfloat16


def split2(x):
    high = x.astype(BF16)
    low = (x - high.astype(F32)).astype(BF16)
    return jnp.concatenate([high, low], axis=0)


def pick(x, onehot):
    rows = x.shape[0]
    both = jnp.dot(split2(x), onehot, preferred_element_type=F32)
    return both[:rows] + both[rows:]


def place(x, onehot):
    rows = x.shape[0]
    both = lax.dot_general(
        split2(x), onehot, (((1,), (1,)), ((), ())), preferred_element_type=F32
    )
    return both[:rows] + both[rows:]


def onehot_of(index_row, height):
    iota = lax.broadcasted_iota(jnp.int32, (height, index_row.shape[1]), 0)
    return jnp.where(iota == index_row, 1.0, 0.0).astype(BF16)


def row_iota(width):
    return lax.broadcasted_iota(jnp.int32, (1, width), 1)


def kernel(
    n,
    rs_ref,
    sigma_ref,
    nu_ref,
    curl_hbm,
    pat_ref,
    cw_ref,
    meta_ref,
    x_ref,
    r_ref,
    curl,
    oh_pat,
    oh_blk,
    oh_nbr,
    oh_coil,
    picked,
    back,
    dacc,
    cw_nbr,
    meta_nbr,
    msg,
    msg_in,
    row,
    row_in,
    curl_sem,
    cond_send,
    cond_recv,
    msg_send,
    msg_recv,
    row_send,
    row_recv,
):
    faces, width = nu_ref.shape
    kinds = pat_ref.shape[0]
    rows = cw_ref.shape[1]
    me = lax.axis_index("dom")
    nxt = jnp.where(me == n - 1, 0, me + 1)
    prv = jnp.where(me == 0, n - 1, me - 1)

    def at(offset):
        target = me + offset
        return jnp.where(target >= n, target - n, target)

    barrier = pltpu.get_barrier_semaphore()

    def greet(offset, carry):
        pl.semaphore_signal(barrier, inc=1, device_id=(at(offset),), device_id_type=MESH)
        return carry

    lax.fori_loop(1, n, greet, 0)

    steps = faces // 8

    def curl_copy(step):
        part = pl.ds(step * 8, 8)
        return pltpu.make_async_copy(curl_hbm.at[:, part], curl.at[:, part], curl_sem.at[step])

    for step in range(steps):
        curl_copy(step).start()

    lane = row_iota(LANES)
    own_edge = (lane < 32) | (lane >= 96)
    low_edge = lane < 32
    high_edge = lane >= 96
    has_prev = me > 0
    has_next = me < n - 1
    halo_next = (lane >= 32) & (lane < 64) & has_next
    halo_prev = (lane >= 64) & (lane < 96) & has_prev
    halo_lanes = halo_next | halo_prev

    block_row = meta_ref[0:1, :].astype(jnp.int32)
    coil_row = meta_ref[1:2, :].astype(jnp.int32)
    inv_res = meta_ref[2:3, 0:LANES]
    source = meta_ref[3:4, 0:LANES]
    oh_blk[...] = onehot_of(block_row, LANES)
    oh_coil[...] = onehot_of(coil_row, LANES)

    def coil_rows(coil_values):
        wide = jnp.broadcast_to(coil_values, (16, LANES))
        high = wide.astype(BF16)
        rest = wide - high.astype(F32)
        mid = rest.astype(BF16)
        low = (rest - mid.astype(F32)).astype(BF16)
        parts = jnp.dot(
            jnp.concatenate([high, mid, low], axis=0), oh_coil[...], preferred_element_type=F32
        )
        return (parts[0:16] + parts[16:32] + parts[32:48])[0:1]

    def coupled(coil_values):
        return place(cw_ref[...] * coil_rows(coil_values), oh_blk[...])

    rhs = rs_ref[...] + coupled(source)

    coil_iota = lax.broadcasted_iota(jnp.int32, (LANES, LANES), 0)

    def tally(total, weighted, coils):
        for start in range(0, weighted.shape[1], LANES):
            part = weighted[:, start : start + LANES]
            named = coils[:, start : start + LANES]
            total = total + jnp.where(coil_iota == named, part, 0.0)
        return total

    def own_links(field):
        weighted = jnp.sum(cw_ref[...] * pick(field, oh_blk[...]), axis=0, keepdims=True)
        return tally(jnp.zeros((LANES, LANES), F32), weighted, coil_row)

    def as_row(total):
        return jnp.sum(total.T, axis=0, keepdims=True)

    msg[0] = jnp.where(own_edge, rhs, 0.0)
    row[0] = as_row(own_links(rhs))

    pl.semaphore_wait(barrier, n - 1)

    def sides(stage):
        return [
            pltpu.make_async_remote_copy(
                src_ref=msg.at[stage],
                dst_ref=msg_in.at[stage, side],
                send_sem=msg_send.at[stage, side],
                recv_sem=msg_recv.at[stage, side],
                device_id=(target,),
                device_id_type=MESH,
            )
            for side, target in ((0, nxt), (1, prv))
        ]

    def send(stage):
        for copy in sides(stage):
            copy.start()

        def one(offset, carry):
            pltpu.make_async_remote_copy(
                src_ref=row.at[stage],
                dst_ref=row_in.at[stage, offset - 1],
                send_sem=row_send.at[stage],
                recv_sem=row_recv.at[stage],
                device_id=(at(offset),),
                device_id_type=MESH,
            ).start()
            return carry

        lax.fori_loop(1, n, one, 0)

    def receive(stage):
        for copy in sides(stage):
            copy.wait()
        whole = row_in.at[stage]
        pltpu.make_async_copy(whole, whole, row_recv.at[stage]).wait()
        pltpu.make_async_copy(whole, whole, row_send.at[stage]).wait()
        from_prev = pltpu.roll(msg_in[stage, 0], LANES - 32, 1)
        from_next = pltpu.roll(msg_in[stage, 1], 32, 1)
        links = row[stage] + jnp.sum(row_in[stage], axis=0)
        return from_prev, from_next, links

    cond_copies = []
    for side, target in ((0, nxt), (1, prv)):
        for kind, (source_ref, dest_ref) in enumerate(((cw_ref, cw_nbr), (meta_ref, meta_nbr))):
            cond_copies.append(
                pltpu.make_async_remote_copy(
                    src_ref=source_ref,
                    dst_ref=dest_ref.at[side],
                    send_sem=cond_send.at[side, kind],
                    recv_sem=cond_recv.at[side, kind],
                    device_id=(target,),
                    device_id_type=MESH,
                )
            )

    send(0)
    for copy in cond_copies:
        copy.start()

    for k in range(kinds):
        named = pat_ref[k : k + 1, :]
        place_of = jnp.where(named < 32, named + 192, jnp.where(named < 160, named - 32, named))
        oh_pat[:, k * width : (k + 1) * width] = onehot_of(place_of, 2 * LANES)

    from_prev, from_next, links_r = receive(0)
    r = rhs
    r_halo = jnp.where(halo_next, from_next, jnp.where(halo_prev, from_prev, 0.0))
    x = jnp.zeros_like(r)
    p = s = s_halo = links_s = None
    rr_old = alpha = None

    for turn in range(ITERS):
        picked[...] = pick(jnp.concatenate([r, r_halo], axis=1), oh_pat[...])
        back[...] = jnp.zeros_like(back)
        dacc[...] = jnp.zeros_like(dacc)

        def faces_step(step, carry, turn=turn):
            if turn == 0:
                curl_copy(step).wait()
            start = pl.multiple_of(step * 8, 8)
            part = pl.ds(start, 8)
            flux = jnp.zeros((8, 8, width), F32)
            for k in range(kinds):
                for b in range(0, faces, 8):
                    seen = picked[b : b + 8, k * width : (k + 1) * width]
                    flux = flux + curl[k, part, b : b + 8, :] * seen[None]
            face = jnp.sum(flux, axis=1)
            weighted = nu_ref[part, :] * face
            dacc[...] += weighted * face
            wide = jnp.broadcast_to(weighted[:, None, :], (8, 8, width))
            for k in range(kinds):
                for b in range(0, faces, 8):
                    term = jnp.sum(curl[k, part, b : b + 8, :] * wide, axis=0)
                    back[b : b + 8, k * width : (k + 1) * width] += term
            return carry

        lax.fori_loop(0, steps, faces_step, 0)
        spread = place(back[...], oh_pat[...])
        spread_halo = jnp.where(halo_lanes, spread[:, LANES:], 0.0)
        sigma_r = sigma_ref[...] * r
        centre = sigma_r + spread[:, :LANES] + coupled(links_r * inv_res)
        msg[turn + 1] = jnp.where(own_edge, centre, spread_halo)
        rr_lanes = jnp.sum(r * r, axis=0, keepdims=True)
        rar_lanes = jnp.sum(sigma_r * r, axis=0, keepdims=True) + jnp.sum(
            dacc[...], axis=0, keepdims=True
        )
        if turn == 0:
            for copy in cond_copies:
                copy.wait()
            prev_block = meta_nbr[0, 0:1, :].astype(jnp.int32)
            next_block = meta_nbr[1, 0:1, :].astype(jnp.int32)
            prev_lane = jnp.where(prev_block >= 96, prev_block - 32, -1)
            next_lane = jnp.where(next_block < 32, next_block + 32, -1)
            oh_nbr[:, 0:rows] = onehot_of(prev_lane, LANES)
            oh_nbr[:, rows : 2 * rows] = onehot_of(next_lane, LANES)
        if turn + 1 < ITERS:
            total = own_links(centre)
            seen = pick(spread_halo, oh_nbr[...])
            for side in range(2):
                weighted = jnp.sum(
                    cw_nbr[side] * seen[:, side * rows : (side + 1) * rows], axis=0, keepdims=True
                )
                total = tally(total, weighted, meta_nbr[side, 1:2, :].astype(jnp.int32))
        else:
            total = jnp.zeros((LANES, LANES), F32)
        total = jnp.where(coil_iota == RR_ROW, rr_lanes, total)
        total = jnp.where(coil_iota == RAR_ROW, rar_lanes, total)
        row[turn + 1] = as_row(total)
        send(turn + 1)
        from_prev, from_next, links_q = receive(turn + 1)
        q = (
            centre
            + jnp.where(low_edge & has_prev, from_prev, 0.0)
            + jnp.where(high_edge & has_next, from_next, 0.0)
        )
        q_halo = spread_halo + jnp.where(
            halo_next, from_next, jnp.where(halo_prev, from_prev, 0.0)
        )
        rr = jnp.sum(jnp.where(lane == RR_ROW, links_q, 0.0), axis=1, keepdims=True)
        rar = jnp.sum(
            jnp.where(lane == RAR_ROW, links_q, links_r * links_r * inv_res),
            axis=1,
            keepdims=True,
        )
        if turn == 0:
            p, s, s_halo, links_s = r, q, q_halo, links_q
            alpha = rr / rar
        else:
            beta = rr / rr_old
            p = r + beta * p
            s = q + beta * s
            s_halo = q_halo + beta * s_halo
            links_s = links_q + beta * links_s
            alpha = rr / (rar - beta * rr / alpha)
        rr_old = rr
        x = x + alpha * p
        r = r - alpha * s
        r_halo = r_halo - alpha * s_halo
        links_r = links_r - alpha * links_s
    x_ref[...] = x
    r_ref[...] = r


def body(
    right_side,
    sigma,
    reluctivity,
    curl_blocks,
    pattern,
    cond_weight,
    cond_block,
    cond_coil,
    coil_phase,
    coil_resistance,
    switch_state,
):
    n = lax.axis_size("dom")
    width, count = right_side.shape
    kinds = pattern.shape[0]
    rows = cond_weight.shape[1]
    coils = coil_resistance.shape[0]
    states = switch_state.astype(F32)
    volts_of = states - jnp.mean(states)
    volts = jnp.zeros((coils,), F32)
    for phase in range(switch_state.shape[0]):
        volts = jnp.where(coil_phase == phase, LINK_SCALE * volts_of[phase], volts)
    pad = (0, rows - coils)
    meta = jnp.stack(
        [
            cond_block.astype(F32),
            cond_coil[:, 0].astype(F32),
            jnp.pad(1.0 / coil_resistance, pad),
            jnp.pad(volts / coil_resistance, pad),
        ]
        + [jnp.zeros((rows,), F32)] * 4
    )
    vmem = pl.BlockSpec(memory_space=pltpu.VMEM)
    stages = ITERS + 1
    shape = jax.ShapeDtypeStruct((width, count), F32)
    dma = pltpu.SemaphoreType.DMA
    return pl.pallas_call(
        functools.partial(kernel, n),
        out_shape=(shape, shape),
        in_specs=[vmem, vmem, vmem, pl.BlockSpec(memory_space=pl.ANY), vmem, vmem, vmem],
        out_specs=(vmem, vmem),
        scratch_shapes=[
            pltpu.VMEM(curl_blocks.shape, F32),
            pltpu.VMEM((2 * LANES, kinds * count), BF16),
            pltpu.VMEM((LANES, rows), BF16),
            pltpu.VMEM((LANES, 2 * rows), BF16),
            pltpu.VMEM((LANES, rows), BF16),
            pltpu.VMEM((width, kinds * count), F32),
            pltpu.VMEM((width, kinds * count), F32),
            pltpu.VMEM((8, count), F32),
            pltpu.VMEM((2, width, rows), F32),
            pltpu.VMEM((2, 8, rows), F32),
            pltpu.VMEM((stages, width, LANES), F32),
            pltpu.VMEM((stages, 2, width, LANES), F32),
            pltpu.VMEM((stages, 1, LANES), F32),
            pltpu.VMEM((stages, n - 1, 1, LANES), F32),
            dma((width // 8,)),
            dma((2, 2)),
            dma((2, 2)),
            dma((stages, 2)),
            dma((stages, 2)),
            dma((stages,)),
            dma((stages,)),
        ],
        compiler_params=pltpu.CompilerParams(
            collective_id=0, has_side_effects=True, vmem_limit_bytes=40 * 1024 * 1024
        ),
        cost_estimate=pl.CostEstimate(
            flops=4 * ITERS * curl_blocks.size, bytes_accessed=4 * curl_blocks.size, transcendentals=0
        ),
    )(right_side, sigma, reluctivity, curl_blocks, pattern, cond_weight, meta)


def solution(mesh):
    return jax.shard_map(
        body,
        mesh=mesh,
        in_specs=(
            P(None, "dom"),
            P(None, "dom"),
            P(None, "dom"),
            P(None, None, None, "dom"),
            P(None, "dom"),
            P(None, "dom"),
            P("dom"),
            P("dom", None),
            P(),
            P(),
            P(),
        ),
        out_specs=(P(None, "dom"), P(None, "dom")),
        check_vma=False,
    )
```

```python
import functools

import jax
import jax.numpy as jnp
from jax import lax
from jax.experimental import pallas as pl
from jax.experimental.pallas import tpu as pltpu
from jax.sharding import PartitionSpec as P

ITERS = 3
LINK_SCALE = 16.0
LANES = 128
RR_ROW = 126
RAR_ROW = 127
MESH = pl.DeviceIdType.MESH
F32 = jnp.float32
BF16 = jnp.bfloat16


def split2(x):
    high = x.astype(BF16)
    low = (x - high.astype(F32)).astype(BF16)
    return jnp.concatenate([high, low], axis=0)


def pick(x, onehot):
    rows = x.shape[0]
    both = jnp.dot(split2(x), onehot, preferred_element_type=F32)
    return both[:rows] + both[rows:]


def place(x, onehot):
    rows = x.shape[0]
    both = lax.dot_general(
        split2(x), onehot, (((1,), (1,)), ((), ())), preferred_element_type=F32
    )
    return both[:rows] + both[rows:]


def onehot_of(index_row, height):
    iota = lax.broadcasted_iota(jnp.int32, (height, index_row.shape[1]), 0)
    return jnp.where(iota == index_row, 1.0, 0.0).astype(BF16)


def row_iota(width):
    return lax.broadcasted_iota(jnp.int32, (1, width), 1)


def kernel(
    n,
    rs_hbm,
    sigma_hbm,
    nu_hbm,
    curl_hbm,
    pat_hbm,
    cw_hbm,
    blk_hbm,
    coil_hbm,
    phase_hbm,
    res_hbm,
    state_hbm,
    out_ref,
    rs_ref,
    sigma_ref,
    nu_ref,
    pat_ref,
    cw_ref,
    blk_ref,
    coil_ref,
    phase_ref,
    res_ref,
    state_ref,
    curl,
    oh_pat,
    oh_blk,
    oh_nbr,
    oh_coil,
    picked,
    back,
    face_buf,
    coil_buf,
    cw_nbr,
    blk_nbr,
    coil_nbr,
    msg,
    msg_in,
    row,
    row_in,
    load_sem,
    curl_sem,
    cond_send,
    cond_recv,
    msg_send,
    msg_recv,
    row_send,
    row_recv,
):
    faces, width = nu_ref.shape
    kinds = pat_ref.shape[0]
    rows = cw_ref.shape[1]
    me = lax.axis_index("dom")
    nxt = jnp.where(me == n - 1, 0, me + 1)
    prv = jnp.where(me == 0, n - 1, me - 1)

    def at(offset):
        target = me + offset
        return jnp.where(target >= n, target - n, target)

    barrier = pltpu.get_barrier_semaphore()

    def greet(offset, carry):
        pl.semaphore_signal(barrier, inc=1, device_id=(at(offset),), device_id_type=MESH)
        return carry

    lax.fori_loop(1, n, greet, 0)

    steps = faces // 8

    def curl_copy(step):
        part = pl.ds(step * 8, 8)
        return pltpu.make_async_copy(curl_hbm.at[:, part], curl.at[:, part], curl_sem.at[step])

    loads = [
        pltpu.make_async_copy(source_ref, dest_ref, load_sem.at[i])
        for i, (source_ref, dest_ref) in enumerate(
            (
                (blk_hbm, blk_ref),
                (coil_hbm, coil_ref),
                (phase_hbm, phase_ref),
                (res_hbm, res_ref),
                (state_hbm, state_ref),
                (cw_hbm, cw_ref),
                (rs_hbm, rs_ref),
                (pat_hbm, pat_ref),
                (sigma_hbm, sigma_ref),
                (nu_hbm, nu_ref),
            )
        )
    ]
    for copy in loads:
        copy.start()
    for step in range(steps):
        curl_copy(step).start()
    coil_buf[...] = jnp.zeros_like(coil_buf)
    for copy in loads:
        copy.wait()

    lane = row_iota(LANES)
    own_edge = (lane < 32) | (lane >= 96)
    low_edge = lane < 32
    high_edge = lane >= 96
    has_prev = me > 0
    has_next = me < n - 1
    halo_next = (lane >= 32) & (lane < 64) & has_next
    halo_prev = (lane >= 64) & (lane < 96) & has_prev
    halo_lanes = halo_next | halo_prev

    block_row = blk_ref[...]
    coil_row = coil_ref[...]
    states = state_ref[...].astype(F32)
    phases = states.shape[1]
    centred = LINK_SCALE * (states - jnp.sum(states, axis=1, keepdims=True) / phases)
    volts = jnp.zeros(res_ref.shape, F32)
    for phase in range(phases):
        volts = jnp.where(phase_ref[...] == phase, centred[:, phase : phase + 1], volts)
    coils = res_ref.shape[1]
    coil_buf[0, :, 0:coils] = 1.0 / res_ref[...]
    coil_buf[1, :, 0:coils] = volts / res_ref[...]
    inv_res = coil_buf[0]
    source = coil_buf[1]
    oh_blk[...] = onehot_of(block_row, LANES)
    oh_coil[...] = onehot_of(coil_row, LANES)

    def coil_rows(coil_values):
        wide = jnp.broadcast_to(coil_values, (16, LANES))
        high = wide.astype(BF16)
        rest = wide - high.astype(F32)
        mid = rest.astype(BF16)
        low = (rest - mid.astype(F32)).astype(BF16)
        parts = jnp.dot(
            jnp.concatenate([high, mid, low], axis=0), oh_coil[...], preferred_element_type=F32
        )
        return (parts[0:16] + parts[16:32] + parts[32:48])[0:1]

    def coupled(coil_values):
        return place(cw_ref[...] * coil_rows(coil_values), oh_blk[...])

    rhs = rs_ref[...] + coupled(source)

    coil_iota = lax.broadcasted_iota(jnp.int32, (LANES, LANES), 0)

    def tally(total, weighted, coils):
        for start in range(0, weighted.shape[1], LANES):
            part = weighted[:, start : start + LANES]
            named = coils[:, start : start + LANES]
            total = total + jnp.where(coil_iota == named, part, 0.0)
        return total

    def own_links(field):
        weighted = jnp.sum(cw_ref[...] * pick(field, oh_blk[...]), axis=0, keepdims=True)
        return tally(jnp.zeros((LANES, LANES), F32), weighted, coil_row)

    def as_row(total):
        return jnp.sum(total.T, axis=0, keepdims=True)

    def sides(stage):
        return [
            pltpu.make_async_remote_copy(
                src_ref=msg.at[stage],
                dst_ref=msg_in.at[stage, side],
                send_sem=msg_send.at[stage, side],
                recv_sem=msg_recv.at[stage, side],
                device_id=(target,),
                device_id_type=MESH,
            )
            for side, target in ((0, nxt), (1, prv))
        ]

    def send_sides(stage):
        for copy in sides(stage):
            copy.start()

    def send_rows(stage):
        def one(offset, carry):
            pltpu.make_async_remote_copy(
                src_ref=row.at[stage],
                dst_ref=row_in.at[stage, offset - 1],
                send_sem=row_send.at[stage],
                recv_sem=row_recv.at[stage],
                device_id=(at(offset),),
                device_id_type=MESH,
            ).start()
            return carry

        lax.fori_loop(1, n, one, 0)

    def receive_sides(stage):
        for copy in sides(stage):
            copy.wait()
        return pltpu.roll(msg_in[stage, 0], LANES - 32, 1), pltpu.roll(msg_in[stage, 1], 32, 1)

    def receive_rows(stage):
        whole = row_in.at[stage]
        pltpu.make_async_copy(whole, whole, row_recv.at[stage]).wait()
        pltpu.make_async_copy(whole, whole, row_send.at[stage]).wait()
        return row[stage] + jnp.sum(row_in[stage], axis=0)

    def at_halo(from_prev, from_next):
        return jnp.where(halo_next, from_next, jnp.where(halo_prev, from_prev, 0.0))

    cond_copies = []
    for side, target in ((0, nxt), (1, prv)):
        for kind, (source_ref, dest_ref) in enumerate(
            ((cw_ref, cw_nbr), (blk_ref, blk_nbr), (coil_ref, coil_nbr))
        ):
            cond_copies.append(
                pltpu.make_async_remote_copy(
                    src_ref=source_ref,
                    dst_ref=dest_ref.at[side],
                    send_sem=cond_send.at[side, kind],
                    recv_sem=cond_recv.at[side, kind],
                    device_id=(target,),
                    device_id_type=MESH,
                )
            )

    def apply(field, halo, first):
        picked[...] = pick(jnp.concatenate([field, halo], axis=1), oh_pat[...])
        back[...] = jnp.zeros_like(back)

        def faces_step(step, carry):
            if first:
                curl_copy(step).wait()
            part = pl.ds(pl.multiple_of(step * 8, 8), 8)
            flux = jnp.zeros((8, 8, width), F32)
            for k in range(kinds):
                for b in range(0, faces, 8):
                    seen = picked[b : b + 8, k * width : (k + 1) * width]
                    flux = flux + curl[k, part, b : b + 8, :] * seen[None]
            face = jnp.sum(flux, axis=1)
            face_buf[part, :] = face
            weighted = nu_ref[part, :] * face
            wide = jnp.broadcast_to(weighted[:, None, :], (8, 8, width))
            for k in range(kinds):
                for b in range(0, faces, 8):
                    term = jnp.sum(curl[k, part, b : b + 8, :] * wide, axis=0)
                    back[b : b + 8, k * width : (k + 1) * width] += term
            return carry

        lax.fori_loop(0, steps, faces_step, 0)
        spread = place(back[...], oh_pat[...])
        return face_buf[...], spread[:, :LANES], jnp.where(halo_lanes, spread[:, LANES:], 0.0)

    msg[0] = jnp.where(own_edge, rhs, 0.0)
    pl.semaphore_wait(barrier, n - 1)
    send_sides(0)
    row[0] = as_row(own_links(rhs))
    send_rows(0)
    for copy in cond_copies:
        copy.start()
    for k in range(kinds):
        named = pat_ref[k : k + 1, :]
        place_of = jnp.where(named < 32, named + 192, jnp.where(named < 160, named - 32, named))
        oh_pat[:, k * width : (k + 1) * width] = onehot_of(place_of, 2 * LANES)

    r = rhs
    r_face, r_spread, r_spread_halo = apply(r, at_halo(*receive_sides(0)), True)
    links_r = receive_rows(0)
    x = jnp.zeros_like(r)

    for copy in cond_copies:
        copy.wait()
    prev_lane = jnp.where(blk_nbr[0] >= 96, blk_nbr[0] - 32, -1)
    next_lane = jnp.where(blk_nbr[1] < 32, blk_nbr[1] + 32, -1)
    oh_nbr[:, 0:rows] = onehot_of(prev_lane, LANES)
    oh_nbr[:, rows : 2 * rows] = onehot_of(next_lane, LANES)

    for turn in range(ITERS):
        last = turn + 1 == ITERS
        sigma_r = sigma_ref[...] * r
        rr_lanes = jnp.sum(r * r, axis=0, keepdims=True)
        rar_lanes = jnp.sum(sigma_r * r + nu_ref[...] * r_face * r_face, axis=0, keepdims=True)

        def send_total(total, turn=turn, rr_lanes=rr_lanes, rar_lanes=rar_lanes):
            total = jnp.where(coil_iota == RR_ROW, rr_lanes, total)
            total = jnp.where(coil_iota == RAR_ROW, rar_lanes, total)
            row[turn + 1] = as_row(total)
            send_rows(turn + 1)

        if last:
            send_total(jnp.zeros((LANES, LANES), F32))
        centre = sigma_r + r_spread + coupled(links_r * inv_res)
        msg[turn + 1] = jnp.where(own_edge, centre, r_spread_halo)
        send_sides(turn + 1)
        if not last:
            total = own_links(centre)
            seen = pick(r_spread_halo, oh_nbr[...])
            for side in range(2):
                weighted = jnp.sum(
                    cw_nbr[side] * seen[:, side * rows : (side + 1) * rows], axis=0, keepdims=True
                )
                total = tally(total, weighted, coil_nbr[side])
            send_total(total)
        from_prev, from_next = receive_sides(turn + 1)
        q = (
            centre
            + jnp.where(low_edge & has_prev, from_prev, 0.0)
            + jnp.where(high_edge & has_next, from_next, 0.0)
        )
        if not last:
            q_halo = r_spread_halo + at_halo(from_prev, from_next)
            q_face, q_spread, q_spread_halo = apply(q, q_halo, False)
        links_q = receive_rows(turn + 1)
        rr = jnp.sum(jnp.where(lane == RR_ROW, links_q, 0.0), axis=1, keepdims=True)
        rar = jnp.sum(
            jnp.where(lane == RAR_ROW, links_q, links_r * links_r * inv_res),
            axis=1,
            keepdims=True,
        )
        if turn == 0:
            p, s, links_s = r, q, links_q
            s_face, s_spread, s_spread_halo = q_face, q_spread, q_spread_halo
            alpha = rr / rar
        else:
            beta = rr / rr_old
            p = r + beta * p
            s = q + beta * s
            alpha = rr / (rar - beta * rr / alpha)
            if not last:
                links_s = links_q + beta * links_s
                s_face = q_face + beta * s_face
                s_spread = q_spread + beta * s_spread
                s_spread_halo = q_spread_halo + beta * s_spread_halo
        rr_old = rr
        x = x + alpha * p
        r = r - alpha * s
        if not last:
            links_r = links_r - alpha * links_s
            r_face = r_face - alpha * s_face
            r_spread = r_spread - alpha * s_spread
            r_spread_halo = r_spread_halo - alpha * s_spread_halo
    out_ref[0:faces, :] = x
    out_ref[faces : 2 * faces, :] = r


def body(
    right_side,
    sigma,
    reluctivity,
    curl_blocks,
    pattern,
    cond_weight,
    cond_block,
    cond_coil,
    coil_phase,
    coil_resistance,
    switch_state,
):
    n = lax.axis_size("dom")
    width, count = right_side.shape
    kinds = pattern.shape[0]
    rows = cond_weight.shape[1]
    vmem = pl.BlockSpec(memory_space=pltpu.VMEM)
    stages = ITERS + 1
    one_row = lambda array: array.reshape(1, -1)
    small = [one_row(array) for array in (cond_block, cond_coil, coil_phase, coil_resistance, switch_state)]
    arrays = [right_side, sigma, reluctivity, curl_blocks, pattern, cond_weight] + small
    loaded = [array for array in arrays if array is not curl_blocks]
    dma = pltpu.SemaphoreType.DMA
    out = pl.pallas_call(
        functools.partial(kernel, n),
        out_shape=jax.ShapeDtypeStruct((2 * width, count), F32),
        in_specs=[pl.BlockSpec(memory_space=pl.ANY)] * len(arrays),
        out_specs=vmem,
        scratch_shapes=[pltpu.VMEM(array.shape, array.dtype) for array in loaded]
        + [
            pltpu.VMEM(curl_blocks.shape, F32),
            pltpu.VMEM((2 * LANES, kinds * count), BF16),
            pltpu.VMEM((LANES, rows), BF16),
            pltpu.VMEM((LANES, 2 * rows), BF16),
            pltpu.VMEM((LANES, rows), BF16),
            pltpu.VMEM((width, kinds * count), F32),
            pltpu.VMEM((width, kinds * count), F32),
            pltpu.VMEM((width, count), F32),
            pltpu.VMEM((2, 1, LANES), F32),
            pltpu.VMEM((2, width, rows), F32),
            pltpu.VMEM((2, 1, rows), jnp.int32),
            pltpu.VMEM((2, 1, rows), jnp.int32),
            pltpu.VMEM((stages, width, LANES), F32),
            pltpu.VMEM((stages, 2, width, LANES), F32),
            pltpu.VMEM((stages, 1, LANES), F32),
            pltpu.VMEM((stages, n - 1, 1, LANES), F32),
            dma((len(loaded),)),
            dma((width // 8,)),
            dma((2, 3)),
            dma((2, 3)),
            dma((stages, 2)),
            dma((stages, 2)),
            dma((stages,)),
            dma((stages,)),
        ],
        compiler_params=pltpu.CompilerParams(
            collective_id=0, has_side_effects=True, vmem_limit_bytes=60 * 1024 * 1024
        ),
        cost_estimate=pl.CostEstimate(
            flops=4 * ITERS * curl_blocks.size, bytes_accessed=4 * curl_blocks.size, transcendentals=0
        ),
    )(*arrays)
    return out[:width], out[width:]


def solution(mesh):
    return jax.shard_map(
        body,
        mesh=mesh,
        in_specs=(
            P(None, "dom"),
            P(None, "dom"),
            P(None, "dom"),
            P(None, None, None, "dom"),
            P(None, "dom"),
            P(None, "dom"),
            P("dom"),
            P("dom", None),
            P(),
            P(),
            P(),
        ),
        out_specs=(P(None, "dom"), P(None, "dom")),
        check_vma=False,
    )
```

```python
import functools

import jax
import jax.numpy as jnp
from jax import lax
from jax.experimental import pallas as pl
from jax.experimental.pallas import tpu as pltpu
from jax.sharding import PartitionSpec as P

ITERS = 3
LINK_SCALE = 16.0
LANES = 128
STEP = 16
RR_ROW = 126
RAR_ROW = 127
MESH = pl.DeviceIdType.MESH
F32 = jnp.float32
BF16 = jnp.bfloat16


def split2(x):
    high = x.astype(BF16)
    low = (x - high.astype(F32)).astype(BF16)
    return jnp.concatenate([high, low], axis=0)


def pick(x, onehot):
    rows = x.shape[0]
    both = jnp.dot(split2(x), onehot, preferred_element_type=F32)
    return both[:rows] + both[rows:]


def onehot_of(index_row, height):
    iota = lax.broadcasted_iota(jnp.int32, (height, index_row.shape[1]), 0)
    return jnp.where(iota == index_row, 1.0, 0.0).astype(BF16)


def onehot_across(index_column, width):
    iota = lax.broadcasted_iota(jnp.int32, (index_column.shape[0], width), 1).astype(F32)
    return jnp.where(iota == index_column, 1.0, 0.0).astype(BF16)


def row_iota(width):
    return lax.broadcasted_iota(jnp.int32, (1, width), 1)


def kernel(
    n,
    rs_hbm,
    sigma_hbm,
    nu_hbm,
    curl_hbm,
    pat_hbm,
    cw_hbm,
    blk_hbm,
    coil_hbm,
    phase_hbm,
    res_hbm,
    state_hbm,
    out_ref,
    rs_ref,
    sigma_ref,
    nu_ref,
    pat_ref,
    cw_ref,
    blk_ref,
    coil_ref,
    phase_ref,
    res_ref,
    state_ref,
    curl,
    oh_pat,
    oh_pat_t,
    oh_blk,
    oh_blk_t,
    oh_nbr,
    oh_coil,
    picked,
    back,
    face_buf,
    coil_buf,
    cw_nbr,
    blk_nbr,
    coil_nbr,
    msg,
    msg_in,
    row,
    row_in,
    load_sem,
    curl_sem,
    cond_send,
    cond_recv,
    msg_send,
    msg_recv,
    row_send,
    row_recv,
):
    faces, width = nu_ref.shape
    kinds = pat_ref.shape[0]
    rows = cw_ref.shape[1]
    me = lax.axis_index("dom")
    nxt = jnp.where(me == n - 1, 0, me + 1)
    prv = jnp.where(me == 0, n - 1, me - 1)

    def at(offset):
        target = me + offset
        return jnp.where(target >= n, target - n, target)

    barrier = pltpu.get_barrier_semaphore()

    def greet(offset, carry):
        pl.semaphore_signal(barrier, inc=1, device_id=(at(offset),), device_id_type=MESH)
        return carry

    lax.fori_loop(1, n, greet, 0)

    steps = faces // 8

    def curl_copy(step):
        part = pl.ds(step * 8, 8)
        return pltpu.make_async_copy(curl_hbm.at[:, part], curl.at[:, part], curl_sem.at[step])

    loads = [
        pltpu.make_async_copy(source_ref, dest_ref, load_sem.at[i])
        for i, (source_ref, dest_ref) in enumerate(
            (
                (blk_hbm, blk_ref),
                (coil_hbm, coil_ref),
                (phase_hbm, phase_ref),
                (res_hbm, res_ref),
                (state_hbm, state_ref),
                (cw_hbm, cw_ref),
                (rs_hbm, rs_ref),
                (pat_hbm, pat_ref),
                (sigma_hbm, sigma_ref),
                (nu_hbm, nu_ref),
            )
        )
    ]
    for copy in loads:
        copy.start()
    for step in range(steps):
        curl_copy(step).start()
    coil_buf[...] = jnp.zeros_like(coil_buf)
    for copy in loads:
        copy.wait()

    lane = row_iota(LANES)
    own_edge = (lane < 32) | (lane >= 96)
    low_edge = lane < 32
    high_edge = lane >= 96
    has_prev = me > 0
    has_next = me < n - 1
    halo_next = (lane >= 32) & (lane < 64) & has_next
    halo_prev = (lane >= 64) & (lane < 96) & has_prev
    halo_lanes = halo_next | halo_prev

    block_row = blk_ref[...]
    coil_row = coil_ref[...]
    states = state_ref[...].astype(F32)
    phases = states.shape[1]
    centred = LINK_SCALE * (states - jnp.sum(states, axis=1, keepdims=True) / phases)
    volts = jnp.zeros(res_ref.shape, F32)
    for phase in range(phases):
        volts = jnp.where(phase_ref[...] == phase, centred[:, phase : phase + 1], volts)
    coils = res_ref.shape[1]
    coil_buf[0, :, 0:coils] = 1.0 / res_ref[...]
    coil_buf[1, :, 0:coils] = volts / res_ref[...]
    inv_res = coil_buf[0]
    source = coil_buf[1]
    oh_blk[...] = onehot_of(block_row, LANES)
    block_column = jnp.broadcast_to(block_row, (8, rows)).astype(F32).T
    oh_blk_t[...] = onehot_across(block_column[:, 0:1], LANES)
    oh_coil[...] = onehot_of(coil_row, LANES)

    def coil_rows(coil_values):
        wide = jnp.broadcast_to(coil_values, (16, LANES))
        high = wide.astype(BF16)
        rest = wide - high.astype(F32)
        mid = rest.astype(BF16)
        low = (rest - mid.astype(F32)).astype(BF16)
        parts = jnp.dot(
            jnp.concatenate([high, mid, low], axis=0), oh_coil[...], preferred_element_type=F32
        )
        return (parts[0:16] + parts[16:32] + parts[32:48])[0:1]

    def coupled(coil_values):
        return pick(cw_ref[...] * coil_rows(coil_values), oh_blk_t[...])

    rhs = rs_ref[...] + coupled(source)

    coil_iota = lax.broadcasted_iota(jnp.int32, (LANES, LANES), 0)

    def tally(total, weighted, coils):
        for start in range(0, weighted.shape[1], LANES):
            part = weighted[:, start : start + LANES]
            named = coils[:, start : start + LANES]
            total = total + jnp.where(coil_iota == named, part, 0.0)
        return total

    def own_links(field):
        weighted = jnp.sum(cw_ref[...] * pick(field, oh_blk[...]), axis=0, keepdims=True)
        return tally(jnp.zeros((LANES, LANES), F32), weighted, coil_row)

    def as_row(total):
        return jnp.sum(total.T, axis=0, keepdims=True)

    def sides(stage):
        return [
            pltpu.make_async_remote_copy(
                src_ref=msg.at[stage],
                dst_ref=msg_in.at[stage, side],
                send_sem=msg_send.at[stage, side],
                recv_sem=msg_recv.at[stage, side],
                device_id=(target,),
                device_id_type=MESH,
            )
            for side, target in ((0, nxt), (1, prv))
        ]

    def send_sides(stage):
        for copy in sides(stage):
            copy.start()

    def send_rows(stage):
        def one(offset, carry):
            pltpu.make_async_remote_copy(
                src_ref=row.at[stage],
                dst_ref=row_in.at[stage, offset - 1],
                send_sem=row_send.at[stage],
                recv_sem=row_recv.at[stage],
                device_id=(at(offset),),
                device_id_type=MESH,
            ).start()
            return carry

        if n <= 32:
            for offset in range(1, n):
                one(offset, 0)
        else:
            lax.fori_loop(1, n, one, 0)

    def receive_sides(stage):
        for copy in sides(stage):
            copy.wait()
        return pltpu.roll(msg_in[stage, 0], LANES - 32, 1), pltpu.roll(msg_in[stage, 1], 32, 1)

    def receive_rows(stage):
        whole = row_in.at[stage]
        pltpu.make_async_copy(whole, whole, row_recv.at[stage]).wait()
        pltpu.make_async_copy(whole, whole, row_send.at[stage]).wait()
        return row[stage] + jnp.sum(row_in[stage], axis=0)

    def at_halo(from_prev, from_next):
        return jnp.where(halo_next, from_next, jnp.where(halo_prev, from_prev, 0.0))

    cond_copies = []
    for side, target in ((0, nxt), (1, prv)):
        for kind, (source_ref, dest_ref) in enumerate(
            ((cw_ref, cw_nbr), (blk_ref, blk_nbr), (coil_ref, coil_nbr))
        ):
            cond_copies.append(
                pltpu.make_async_remote_copy(
                    src_ref=source_ref,
                    dst_ref=dest_ref.at[side],
                    send_sem=cond_send.at[side, kind],
                    recv_sem=cond_recv.at[side, kind],
                    device_id=(target,),
                    device_id_type=MESH,
                )
            )

    def apply(field, halo, first):
        picked[...] = pick(jnp.concatenate([field, halo], axis=1), oh_pat[...])
        back[...] = jnp.zeros_like(back)

        def faces_step(step, carry):
            if first:
                for half in range(STEP // 8):
                    curl_copy(step * (STEP // 8) + half).wait()
            part = pl.ds(pl.multiple_of(step * STEP, STEP), STEP)
            flux = jnp.zeros((STEP, 8, width), F32)
            for k in range(kinds):
                for b in range(0, faces, 8):
                    seen = picked[b : b + 8, k * width : (k + 1) * width]
                    flux = flux + curl[k, part, b : b + 8, :] * seen[None]
            face = jnp.sum(flux, axis=1)
            face_buf[part, :] = face
            weighted = nu_ref[part, :] * face
            wide = jnp.broadcast_to(weighted[:, None, :], (STEP, 8, width))
            for k in range(kinds):
                for b in range(0, faces, 8):
                    term = jnp.sum(curl[k, part, b : b + 8, :] * wide, axis=0)
                    back[b : b + 8, k * width : (k + 1) * width] += term
            return carry

        lax.fori_loop(0, faces // STEP, faces_step, 0)
        spread = pick(back[...], oh_pat_t[...])
        return face_buf[...], spread[:, :LANES], jnp.where(halo_lanes, spread[:, LANES:], 0.0)

    msg[0] = jnp.where(own_edge, rhs, 0.0)
    pl.semaphore_wait(barrier, n - 1)
    send_sides(0)
    row[0] = as_row(own_links(rhs))
    send_rows(0)
    for copy in cond_copies:
        copy.start()
    named = pat_ref[...]
    place_of = jnp.where(named < 32, named + 192, jnp.where(named < 160, named - 32, named))
    spare = jnp.zeros((8 - kinds % 8, width), jnp.int32)
    place_column = jnp.concatenate([place_of, spare], axis=0).astype(F32).T
    for k in range(kinds):
        part = slice(k * width, (k + 1) * width)
        oh_pat[:, part] = onehot_of(place_of[k : k + 1, :], 2 * LANES)
        oh_pat_t[part, :] = onehot_across(place_column[:, k : k + 1], 2 * LANES)

    r = rhs
    r_face, r_spread, r_spread_halo = apply(r, at_halo(*receive_sides(0)), True)
    links_r = receive_rows(0)
    x = jnp.zeros_like(r)

    for copy in cond_copies:
        copy.wait()
    prev_lane = jnp.where(blk_nbr[0] >= 96, blk_nbr[0] - 32, -1)
    next_lane = jnp.where(blk_nbr[1] < 32, blk_nbr[1] + 32, -1)
    oh_nbr[:, 0:rows] = onehot_of(prev_lane, LANES)
    oh_nbr[:, rows : 2 * rows] = onehot_of(next_lane, LANES)

    for turn in range(ITERS):
        last = turn + 1 == ITERS
        sigma_r = sigma_ref[...] * r
        rr_lanes = jnp.sum(r * r, axis=0, keepdims=True)
        rar_lanes = jnp.sum(sigma_r * r + nu_ref[...] * r_face * r_face, axis=0, keepdims=True)

        def send_total(total, turn=turn, rr_lanes=rr_lanes, rar_lanes=rar_lanes):
            total = jnp.where(coil_iota == RR_ROW, rr_lanes, total)
            total = jnp.where(coil_iota == RAR_ROW, rar_lanes, total)
            row[turn + 1] = as_row(total)
            send_rows(turn + 1)

        if last:
            send_total(jnp.zeros((LANES, LANES), F32))
        centre = sigma_r + r_spread + coupled(links_r * inv_res)
        msg[turn + 1] = jnp.where(own_edge, centre, r_spread_halo)
        send_sides(turn + 1)
        if not last:
            total = own_links(centre)
            seen = pick(r_spread_halo, oh_nbr[...])
            for side in range(2):
                weighted = jnp.sum(
                    cw_nbr[side] * seen[:, side * rows : (side + 1) * rows], axis=0, keepdims=True
                )
                total = tally(total, weighted, coil_nbr[side])
            send_total(total)
        from_prev, from_next = receive_sides(turn + 1)
        q = (
            centre
            + jnp.where(low_edge & has_prev, from_prev, 0.0)
            + jnp.where(high_edge & has_next, from_next, 0.0)
        )
        if not last:
            q_halo = r_spread_halo + at_halo(from_prev, from_next)
            q_face, q_spread, q_spread_halo = apply(q, q_halo, False)
        links_q = receive_rows(turn + 1)
        rr = jnp.sum(jnp.where(lane == RR_ROW, links_q, 0.0), axis=1, keepdims=True)
        rar = jnp.sum(
            jnp.where(lane == RAR_ROW, links_q, links_r * links_r * inv_res),
            axis=1,
            keepdims=True,
        )
        if turn == 0:
            p, s, links_s = r, q, links_q
            s_face, s_spread, s_spread_halo = q_face, q_spread, q_spread_halo
            alpha = rr / rar
        else:
            beta = rr / rr_old
            p = r + beta * p
            s = q + beta * s
            alpha = rr / (rar - beta * rr / alpha)
            if not last:
                links_s = links_q + beta * links_s
                s_face = q_face + beta * s_face
                s_spread = q_spread + beta * s_spread
                s_spread_halo = q_spread_halo + beta * s_spread_halo
        rr_old = rr
        x = x + alpha * p
        r = r - alpha * s
        if not last:
            links_r = links_r - alpha * links_s
            r_face = r_face - alpha * s_face
            r_spread = r_spread - alpha * s_spread
            r_spread_halo = r_spread_halo - alpha * s_spread_halo
    out_ref[0:faces, :] = x
    out_ref[faces : 2 * faces, :] = r


def body(
    right_side,
    sigma,
    reluctivity,
    curl_blocks,
    pattern,
    cond_weight,
    cond_block,
    cond_coil,
    coil_phase,
    coil_resistance,
    switch_state,
):
    n = lax.axis_size("dom")
    width, count = right_side.shape
    kinds = pattern.shape[0]
    rows = cond_weight.shape[1]
    vmem = pl.BlockSpec(memory_space=pltpu.VMEM)
    stages = ITERS + 1
    one_row = lambda array: array.reshape(1, -1)
    small = [one_row(array) for array in (cond_block, cond_coil, coil_phase, coil_resistance, switch_state)]
    arrays = [right_side, sigma, reluctivity, curl_blocks, pattern, cond_weight] + small
    loaded = [array for array in arrays if array is not curl_blocks]
    dma = pltpu.SemaphoreType.DMA
    out = pl.pallas_call(
        functools.partial(kernel, n),
        out_shape=jax.ShapeDtypeStruct((2 * width, count), F32),
        in_specs=[pl.BlockSpec(memory_space=pl.ANY)] * len(arrays),
        out_specs=vmem,
        scratch_shapes=[pltpu.VMEM(array.shape, array.dtype) for array in loaded]
        + [
            pltpu.VMEM(curl_blocks.shape, F32),
            pltpu.VMEM((2 * LANES, kinds * count), BF16),
            pltpu.VMEM((kinds * count, 2 * LANES), BF16),
            pltpu.VMEM((LANES, rows), BF16),
            pltpu.VMEM((rows, LANES), BF16),
            pltpu.VMEM((LANES, 2 * rows), BF16),
            pltpu.VMEM((LANES, rows), BF16),
            pltpu.VMEM((width, kinds * count), F32),
            pltpu.VMEM((width, kinds * count), F32),
            pltpu.VMEM((width, count), F32),
            pltpu.VMEM((2, 1, LANES), F32),
            pltpu.VMEM((2, width, rows), F32),
            pltpu.VMEM((2, 1, rows), jnp.int32),
            pltpu.VMEM((2, 1, rows), jnp.int32),
            pltpu.VMEM((stages, width, LANES), F32),
            pltpu.VMEM((stages, 2, width, LANES), F32),
            pltpu.VMEM((stages, 1, LANES), F32),
            pltpu.VMEM((stages, n - 1, 1, LANES), F32),
            dma((len(loaded),)),
            dma((width // 8,)),
            dma((2, 3)),
            dma((2, 3)),
            dma((stages, 2)),
            dma((stages, 2)),
            dma((stages,)),
            dma((stages,)),
        ],
        compiler_params=pltpu.CompilerParams(
            collective_id=0, has_side_effects=True, vmem_limit_bytes=60 * 1024 * 1024
        ),
        cost_estimate=pl.CostEstimate(
            flops=4 * ITERS * curl_blocks.size, bytes_accessed=4 * curl_blocks.size, transcendentals=0
        ),
    )(*arrays)
    return out[:width], out[width:]


def solution(mesh):
    return jax.shard_map(
        body,
        mesh=mesh,
        in_specs=(
            P(None, "dom"),
            P(None, "dom"),
            P(None, "dom"),
            P(None, None, None, "dom"),
            P(None, "dom"),
            P(None, "dom"),
            P("dom"),
            P("dom", None),
            P(),
            P(),
            P(),
        ),
        out_specs=(P(None, "dom"), P(None, "dom")),
        check_vma=False,
    )
```

```python
import functools

import jax
import jax.numpy as jnp
from jax import lax
from jax.experimental import pallas as pl
from jax.experimental.pallas import tpu as pltpu
from jax.sharding import PartitionSpec as P

ITERS = 3
LINK_SCALE = 16.0
LANES = 128
STEP = 16
RR_ROW = 126
RAR_ROW = 127
MESH = pl.DeviceIdType.MESH
F32 = jnp.float32
BF16 = jnp.bfloat16


def split2(x):
    high = x.astype(BF16)
    low = (x - high.astype(F32)).astype(BF16)
    return jnp.concatenate([high, low], axis=0)


def pick(x, onehot):
    rows = x.shape[0]
    both = jnp.dot(split2(x), onehot, preferred_element_type=F32)
    return both[:rows] + both[rows:]


def onehot_of(index_row, height):
    iota = lax.broadcasted_iota(jnp.int32, (height, index_row.shape[1]), 0)
    return jnp.where(iota == index_row, 1.0, 0.0).astype(BF16)


def onehot_across(index_column, width):
    iota = lax.broadcasted_iota(jnp.int32, (index_column.shape[0], width), 1).astype(F32)
    return jnp.where(iota == index_column, 1.0, 0.0).astype(BF16)


def row_iota(width):
    return lax.broadcasted_iota(jnp.int32, (1, width), 1)


def kernel(
    n,
    rs_hbm,
    sigma_hbm,
    nu_hbm,
    curl_hbm,
    pat_hbm,
    cw_hbm,
    blk_hbm,
    coil_hbm,
    phase_hbm,
    res_hbm,
    state_hbm,
    out_ref,
    rs_ref,
    sigma_ref,
    nu_ref,
    pat_ref,
    cw_ref,
    blk_ref,
    coil_ref,
    phase_ref,
    res_ref,
    state_ref,
    curl,
    oh_pat,
    oh_pat_t,
    oh_blk,
    oh_blk_t,
    oh_nbr,
    oh_coil,
    picked,
    back,
    face_buf,
    coil_buf,
    cw_nbr,
    blk_nbr,
    coil_nbr,
    msg,
    msg_in,
    row,
    row_in,
    load_sem,
    curl_sem,
    cond_send,
    cond_recv,
    msg_send,
    msg_recv,
    row_send,
    row_recv,
):
    faces, width = nu_ref.shape
    kinds = pat_ref.shape[0]
    rows = cw_ref.shape[1]
    me = lax.axis_index("dom")
    nxt = jnp.where(me == n - 1, 0, me + 1)
    prv = jnp.where(me == 0, n - 1, me - 1)

    def at(offset):
        target = me + offset
        return jnp.where(target >= n, target - n, target)

    barrier = pltpu.get_barrier_semaphore()

    def greet(offset, carry):
        pl.semaphore_signal(barrier, inc=1, device_id=(at(offset),), device_id_type=MESH)
        return carry

    lax.fori_loop(1, n, greet, 0)

    steps = faces // 8

    def curl_copy(step):
        part = pl.ds(step * 8, 8)
        return pltpu.make_async_copy(curl_hbm.at[:, part], curl.at[:, part], curl_sem.at[step])

    loads = [
        pltpu.make_async_copy(source_ref, dest_ref, load_sem.at[i])
        for i, (source_ref, dest_ref) in enumerate(
            (
                (blk_hbm, blk_ref),
                (coil_hbm, coil_ref),
                (phase_hbm, phase_ref),
                (res_hbm, res_ref),
                (state_hbm, state_ref),
                (cw_hbm, cw_ref),
                (rs_hbm, rs_ref),
                (pat_hbm, pat_ref),
                (sigma_hbm, sigma_ref),
                (nu_hbm, nu_ref),
            )
        )
    ]
    for copy in loads:
        copy.start()
    for step in range(steps):
        curl_copy(step).start()
    coil_buf[...] = jnp.zeros_like(coil_buf)
    for copy in loads:
        copy.wait()

    lane = row_iota(LANES)
    own_edge = (lane < 32) | (lane >= 96)
    low_edge = lane < 32
    high_edge = lane >= 96
    has_prev = me > 0
    has_next = me < n - 1
    halo_next = (lane >= 32) & (lane < 64) & has_next
    halo_prev = (lane >= 64) & (lane < 96) & has_prev
    halo_lanes = halo_next | halo_prev

    departs = (has_next, has_prev)
    arrives = (has_prev, has_next)

    def clear(side):
        for stage in range(ITERS + 1):
            msg_in[stage, side] = jnp.zeros(msg_in.shape[2:], F32)
        cw_nbr[side] = jnp.zeros(cw_nbr.shape[1:], F32)
        blk_nbr[side] = jnp.zeros(blk_nbr.shape[1:], jnp.int32)
        coil_nbr[side] = jnp.zeros(coil_nbr.shape[1:], jnp.int32)

    for side in range(2):
        pl.when(jnp.logical_not(arrives[side]))(functools.partial(clear, side))

    block_row = blk_ref[...]
    coil_row = coil_ref[...]
    states = state_ref[...].astype(F32)
    phases = states.shape[1]
    centred = LINK_SCALE * (states - jnp.sum(states, axis=1, keepdims=True) / phases)
    volts = jnp.zeros(res_ref.shape, F32)
    for phase in range(phases):
        volts = jnp.where(phase_ref[...] == phase, centred[:, phase : phase + 1], volts)
    coils = res_ref.shape[1]
    coil_buf[0, :, 0:coils] = 1.0 / res_ref[...]
    coil_buf[1, :, 0:coils] = volts / res_ref[...]
    inv_res = coil_buf[0]
    source = coil_buf[1]
    oh_blk[...] = onehot_of(block_row, LANES)
    block_column = jnp.broadcast_to(block_row, (8, rows)).astype(F32).T
    oh_blk_t[...] = onehot_across(block_column[:, 0:1], LANES)
    oh_coil[...] = onehot_of(coil_row, LANES)

    def coil_rows(coil_values):
        wide = jnp.broadcast_to(coil_values, (16, LANES))
        high = wide.astype(BF16)
        rest = wide - high.astype(F32)
        mid = rest.astype(BF16)
        low = (rest - mid.astype(F32)).astype(BF16)
        parts = jnp.dot(
            jnp.concatenate([high, mid, low], axis=0), oh_coil[...], preferred_element_type=F32
        )
        return (parts[0:16] + parts[16:32] + parts[32:48])[0:1]

    def coupled(coil_values):
        return pick(cw_ref[...] * coil_rows(coil_values), oh_blk_t[...])

    rhs = rs_ref[...] + coupled(source)

    coil_iota = lax.broadcasted_iota(jnp.int32, (LANES, LANES), 0)

    def tally(total, weighted, coils):
        for start in range(0, weighted.shape[1], LANES):
            part = weighted[:, start : start + LANES]
            named = coils[:, start : start + LANES]
            total = total + jnp.where(coil_iota == named, part, 0.0)
        return total

    def own_links(field):
        weighted = jnp.sum(cw_ref[...] * pick(field, oh_blk[...]), axis=0, keepdims=True)
        return tally(jnp.zeros((LANES, LANES), F32), weighted, coil_row)

    def as_row(total):
        return jnp.sum(total.T, axis=0, keepdims=True)

    def sides(stage):
        return [
            pltpu.make_async_remote_copy(
                src_ref=msg.at[stage],
                dst_ref=msg_in.at[stage, side],
                send_sem=msg_send.at[stage, side],
                recv_sem=msg_recv.at[stage, side],
                device_id=(target,),
                device_id_type=MESH,
            )
            for side, target in ((0, nxt), (1, prv))
        ]

    def send_sides(stage):
        for side, copy in enumerate(sides(stage)):
            pl.when(departs[side])(copy.start)

    def send_rows(stage):
        def one(offset, carry):
            pltpu.make_async_remote_copy(
                src_ref=row.at[stage],
                dst_ref=row_in.at[stage, offset - 1],
                send_sem=row_send.at[stage],
                recv_sem=row_recv.at[stage],
                device_id=(at(offset),),
                device_id_type=MESH,
            ).start()
            return carry

        if n <= 32:
            for offset in range(1, n):
                one(offset, 0)
        else:
            lax.fori_loop(1, n, one, 0)

    def receive_sides(stage):
        for side, copy in enumerate(sides(stage)):
            pl.when(arrives[side])(copy.wait_recv)
        return pltpu.roll(msg_in[stage, 0], LANES - 32, 1), pltpu.roll(msg_in[stage, 1], 32, 1)

    def receive_rows(stage):
        whole = row_in.at[stage]
        pltpu.make_async_copy(whole, whole, row_recv.at[stage]).wait()
        return row[stage] + jnp.sum(row_in[stage], axis=0)

    def at_halo(from_prev, from_next):
        return jnp.where(halo_next, from_next, jnp.where(halo_prev, from_prev, 0.0))

    cond_copies = []
    for side, target in ((0, nxt), (1, prv)):
        for kind, (source_ref, dest_ref) in enumerate(
            ((cw_ref, cw_nbr), (blk_ref, blk_nbr), (coil_ref, coil_nbr))
        ):
            cond_copies.append((side,
                pltpu.make_async_remote_copy(
                    src_ref=source_ref,
                    dst_ref=dest_ref.at[side],
                    send_sem=cond_send.at[side, kind],
                    recv_sem=cond_recv.at[side, kind],
                    device_id=(target,),
                    device_id_type=MESH,
                ))
            )

    def apply(field, halo, first):
        picked[...] = pick(jnp.concatenate([field, halo], axis=1), oh_pat[...])
        back[...] = jnp.zeros_like(back)

        def faces_step(step, carry):
            if first:
                for half in range(STEP // 8):
                    curl_copy(step * (STEP // 8) + half).wait()
            part = pl.ds(pl.multiple_of(step * STEP, STEP), STEP)
            flux = jnp.zeros((STEP, 8, width), F32)
            for k in range(kinds):
                for b in range(0, faces, 8):
                    seen = picked[b : b + 8, k * width : (k + 1) * width]
                    flux = flux + curl[k, part, b : b + 8, :] * seen[None]
            face = jnp.sum(flux, axis=1)
            face_buf[part, :] = face
            weighted = nu_ref[part, :] * face
            wide = jnp.broadcast_to(weighted[:, None, :], (STEP, 8, width))
            for k in range(kinds):
                for b in range(0, faces, 8):
                    term = jnp.sum(curl[k, part, b : b + 8, :] * wide, axis=0)
                    back[b : b + 8, k * width : (k + 1) * width] += term
            return carry

        lax.fori_loop(0, faces // STEP, faces_step, 0)

    def gathered():
        spread = pick(back[...], oh_pat_t[...])
        return face_buf[...], spread[:, :LANES], jnp.where(halo_lanes, spread[:, LANES:], 0.0)

    msg[0] = jnp.where(own_edge, rhs, 0.0)
    pl.semaphore_wait(barrier, n - 1)
    send_sides(0)
    row[0] = as_row(own_links(rhs))
    send_rows(0)
    for side, copy in cond_copies:
        pl.when(departs[side])(copy.start)
    named = pat_ref[...]
    place_of = jnp.where(named < 32, named + 192, jnp.where(named < 160, named - 32, named))
    spare = jnp.zeros((8 - kinds % 8, width), jnp.int32)
    place_column = jnp.concatenate([place_of, spare], axis=0).astype(F32).T
    for k in range(kinds):
        part = slice(k * width, (k + 1) * width)
        oh_pat[:, part] = onehot_of(place_of[k : k + 1, :], 2 * LANES)
        oh_pat_t[part, :] = onehot_across(place_column[:, k : k + 1], 2 * LANES)

    r = rhs
    apply(r, at_halo(*receive_sides(0)), True)
    for side, copy in cond_copies:
        pl.when(arrives[side])(copy.wait_recv)
    links_r = receive_rows(0)
    r_face, r_spread, r_spread_halo = gathered()
    x = jnp.zeros_like(r)

    prev_lane = jnp.where(blk_nbr[0] >= 96, blk_nbr[0] - 32, -1)
    next_lane = jnp.where(blk_nbr[1] < 32, blk_nbr[1] + 32, -1)
    oh_nbr[:, 0:rows] = onehot_of(prev_lane, LANES)
    oh_nbr[:, rows : 2 * rows] = onehot_of(next_lane, LANES)

    for turn in range(ITERS):
        last = turn + 1 == ITERS
        sigma_r = sigma_ref[...] * r
        rr_lanes = jnp.sum(r * r, axis=0, keepdims=True)
        rar_lanes = jnp.sum(sigma_r * r + nu_ref[...] * r_face * r_face, axis=0, keepdims=True)

        def send_total(total, turn=turn, rr_lanes=rr_lanes, rar_lanes=rar_lanes):
            total = jnp.where(coil_iota == RR_ROW, rr_lanes, total)
            total = jnp.where(coil_iota == RAR_ROW, rar_lanes, total)
            row[turn + 1] = as_row(total)
            send_rows(turn + 1)

        if last:
            send_total(jnp.zeros((LANES, LANES), F32))
        centre = sigma_r + r_spread + coupled(links_r * inv_res)
        msg[turn + 1] = jnp.where(own_edge, centre, r_spread_halo)
        send_sides(turn + 1)
        if not last:
            total = own_links(centre)
            seen = pick(r_spread_halo, oh_nbr[...])
            for side in range(2):
                weighted = jnp.sum(
                    cw_nbr[side] * seen[:, side * rows : (side + 1) * rows], axis=0, keepdims=True
                )
                total = tally(total, weighted, coil_nbr[side])
            send_total(total)
        from_prev, from_next = receive_sides(turn + 1)
        q = (
            centre
            + jnp.where(low_edge & has_prev, from_prev, 0.0)
            + jnp.where(high_edge & has_next, from_next, 0.0)
        )
        if not last:
            q_halo = r_spread_halo + at_halo(from_prev, from_next)
            apply(q, q_halo, False)
        links_q = receive_rows(turn + 1)
        if not last:
            q_face, q_spread, q_spread_halo = gathered()
        rr = jnp.sum(jnp.where(lane == RR_ROW, links_q, 0.0), axis=1, keepdims=True)
        rar = jnp.sum(
            jnp.where(lane == RAR_ROW, links_q, links_r * links_r * inv_res),
            axis=1,
            keepdims=True,
        )
        if turn == 0:
            p, s, links_s = r, q, links_q
            s_face, s_spread, s_spread_halo = q_face, q_spread, q_spread_halo
            alpha = rr / rar
        else:
            beta = rr / rr_old
            p = r + beta * p
            s = q + beta * s
            alpha = rr / (rar - beta * rr / alpha)
            if not last:
                links_s = links_q + beta * links_s
                s_face = q_face + beta * s_face
                s_spread = q_spread + beta * s_spread
                s_spread_halo = q_spread_halo + beta * s_spread_halo
        rr_old = rr
        x = x + alpha * p
        r = r - alpha * s
        if not last:
            links_r = links_r - alpha * links_s
            r_face = r_face - alpha * s_face
            r_spread = r_spread - alpha * s_spread
            r_spread_halo = r_spread_halo - alpha * s_spread_halo
    out_ref[0:faces, :] = x
    out_ref[faces : 2 * faces, :] = r
    for side, copy in cond_copies:
        pl.when(departs[side])(copy.wait_send)
    for stage in range(ITERS + 1):
        for side, copy in enumerate(sides(stage)):
            pl.when(departs[side])(copy.wait_send)
        whole = row_in.at[stage]
        pltpu.make_async_copy(whole, whole, row_send.at[stage]).wait()


def body(
    right_side,
    sigma,
    reluctivity,
    curl_blocks,
    pattern,
    cond_weight,
    cond_block,
    cond_coil,
    coil_phase,
    coil_resistance,
    switch_state,
):
    n = lax.axis_size("dom")
    width, count = right_side.shape
    kinds = pattern.shape[0]
    rows = cond_weight.shape[1]
    vmem = pl.BlockSpec(memory_space=pltpu.VMEM)
    stages = ITERS + 1
    one_row = lambda array: array.reshape(1, -1)
    small = [one_row(array) for array in (cond_block, cond_coil, coil_phase, coil_resistance, switch_state)]
    arrays = [right_side, sigma, reluctivity, curl_blocks, pattern, cond_weight] + small
    loaded = [array for array in arrays if array is not curl_blocks]
    dma = pltpu.SemaphoreType.DMA
    out = pl.pallas_call(
        functools.partial(kernel, n),
        out_shape=jax.ShapeDtypeStruct((2 * width, count), F32),
        in_specs=[pl.BlockSpec(memory_space=pl.ANY)] * len(arrays),
        out_specs=vmem,
        scratch_shapes=[pltpu.VMEM(array.shape, array.dtype) for array in loaded]
        + [
            pltpu.VMEM(curl_blocks.shape, F32),
            pltpu.VMEM((2 * LANES, kinds * count), BF16),
            pltpu.VMEM((kinds * count, 2 * LANES), BF16),
            pltpu.VMEM((LANES, rows), BF16),
            pltpu.VMEM((rows, LANES), BF16),
            pltpu.VMEM((LANES, 2 * rows), BF16),
            pltpu.VMEM((LANES, rows), BF16),
            pltpu.VMEM((width, kinds * count), F32),
            pltpu.VMEM((width, kinds * count), F32),
            pltpu.VMEM((width, count), F32),
            pltpu.VMEM((2, 1, LANES), F32),
            pltpu.VMEM((2, width, rows), F32),
            pltpu.VMEM((2, 1, rows), jnp.int32),
            pltpu.VMEM((2, 1, rows), jnp.int32),
            pltpu.VMEM((stages, width, LANES), F32),
            pltpu.VMEM((stages, 2, width, LANES), F32),
            pltpu.VMEM((stages, 1, LANES), F32),
            pltpu.VMEM((stages, n - 1, 1, LANES), F32),
            dma((len(loaded),)),
            dma((width // 8,)),
            dma((2, 3)),
            dma((2, 3)),
            dma((stages, 2)),
            dma((stages, 2)),
            dma((stages,)),
            dma((stages,)),
        ],
        compiler_params=pltpu.CompilerParams(
            collective_id=0, has_side_effects=True, vmem_limit_bytes=60 * 1024 * 1024
        ),
        cost_estimate=pl.CostEstimate(
            flops=4 * ITERS * curl_blocks.size, bytes_accessed=4 * curl_blocks.size, transcendentals=0
        ),
    )(*arrays)
    return out[:width], out[width:]


def solution(mesh):
    return jax.shard_map(
        body,
        mesh=mesh,
        in_specs=(
            P(None, "dom"),
            P(None, "dom"),
            P(None, "dom"),
            P(None, None, None, "dom"),
            P(None, "dom"),
            P(None, "dom"),
            P("dom"),
            P("dom", None),
            P(),
            P(),
            P(),
        ),
        out_specs=(P(None, "dom"), P(None, "dom")),
        check_vma=False,
    )
```
